32 devices in a mesh: groups: 2 (over y), set: 4 (over x, core), gy: 4 (over z).
Axes of the slice: x: 2, y: 2, z: 4, core: 2. Of those that a mesh axis runs over, the one named last changes fastest.
Arguments:
- grain_ids: int32 [16, 64, 128], P('groups', 'gy'), parts along dimension 0, may hold values from 0 to 1023, as said below
- colouring: int32 [2048], P('groups'), parts along dimension 0, may hold values from 0 to 15
- mobility: float32 [16, 64, 128], P('groups', 'gy'), parts along dimension 0, may hold values from 0.5 to 2
Outputs:
- level: float32 [32, 8, 64, 128], P(('groups', 'set'), None, 'gy'), parts along dimension 0
The draws below stay inside these ranges and needn't reach their ends.
There are 2 independent parts, one for each index of `groups`. The reference program is written for one: setup_inputs(seed, part) draws one part's arguments, and reference() takes and returns one part's arrays. A program takes and returns all parts, laid end to end along the dimension named above; each array names one. Nothing has to cross between parts.
Inputs may be any that keep to these rules, and one draw needn't show every extreme that they name: `grain_ids`: each cell holds the number of the cube of 4 x 4 x 4 cells in which it lies after each of its coordinates is moved by -1, 0 or 1 cell with periodic wrap; cubes are numbered with z slowest and x fastest.
All inputs are finite; a program needn't handle non-finite values.
Results may differ from the reference program's by a relative error of at most 0.0003.
Values sent between devices are 32-bit elements; how exact they have to be, the bound alone decides.
A program may use at most 64 MiB of HBM per device.

```python
import math
from functools import partial
import jax
import jax.numpy as jnp
from jax import lax

SETS = 16
NX = 128
NZ = 8
STEPS = 2
REINIT = 3
BOX = 4
NY = 64
GRAINS = 1024


def draw_grain_ids(key, part):
    key = jax.random.fold_in(key, 11)
    key_z, key_y, key_x = jax.random.split(key, 3)
    shape = (NZ, NY, NX)
    coord_z = (lax.broadcasted_iota(jnp.int32, shape, 0) + jax.random.randint(key_z, shape, -1, 2)) % NZ
    coord_y = (lax.broadcasted_iota(jnp.int32, shape, 1) + jax.random.randint(key_y, shape, -1, 2)) % NY
    coord_x = (lax.broadcasted_iota(jnp.int32, shape, 2) + jax.random.randint(key_x, shape, -1, 2)) % NX
    return ((coord_z // BOX * (NY // BOX) + coord_y // BOX) * (NX // BOX) + coord_x // BOX).astype(jnp.int32)


def plant(result, rng, low, top_value):
    place = [jax.random.randint(jax.random.fold_in(rng, axis), (), 0, length) for axis, length in enumerate(result.shape)]
    widest = result.shape.index(max(result.shape))
    beside = place[:widest] + [(place[widest] + 1) % result.shape[widest]] + place[widest + 1:]
    return result.at[tuple(place)].set(low).at[tuple(beside)].set(top_value)


def shard_levels(rng, dims, pieces, least, largest):
    level, own = 1.0, jax.random.fold_in(rng, 6)
    for axis_at, parts in pieces:
        heights = jnp.exp(jax.random.uniform(jax.random.fold_in(own, axis_at), (parts,), jnp.float32, least / len(pieces), largest / len(pieces)))
        level = level * jnp.repeat(heights, dims[axis_at] // parts).reshape([-1 if axis == axis_at else 1 for axis in range(len(dims))])
    return level


def setup_inputs(seed: int = 0, part: int = 0) -> dict:
    splits = jax.random.split(jax.random.key(seed), 4)
    own_keys = jax.random.split(jax.random.fold_in(splits[3], part), 4)
    grain_ids = draw_grain_ids(jax.random.fold_in(jax.random.fold_in(splits[3], part), 71), part)
    colouring = plant(jax.random.randint(own_keys[1], (GRAINS,), 0, SETS), jax.random.fold_in(own_keys[1], 1), 0, SETS - 1).astype(jnp.int32)
    mobility = jnp.clip(jnp.exp(math.log(2.0) - 1.3862944 * jax.random.uniform(own_keys[2], (NZ, NY, NX), jnp.float32) ** shard_levels(own_keys[2], (NZ, NY, NX), ((1, 4),), -0.2, 0.2)), 0.5, 2.0)
    return {"grain_ids": grain_ids, "colouring": colouring, "mobility": mobility}


TIME_STEP = 0.08
PSEUDO_STEP = 0.3
WENO_EPS = 1e-06

def squared(value):
    return value * value

def weno_side(diffs):
    far_left, near_left, middle, near_right, far_right = diffs
    smooth_one = 13.0 / 12.0 * squared(far_left - 2.0 * near_left + middle) + 0.25 * squared(far_left - 4.0 * near_left + 3.0 * middle)
    smooth_two = 13.0 / 12.0 * squared(near_left - 2.0 * middle + near_right) + 0.25 * squared(near_left - near_right)
    smooth_three = 13.0 / 12.0 * squared(middle - 2.0 * near_right + far_right) + 0.25 * squared(3.0 * middle - 4.0 * near_right + far_right)
    alpha_one = 0.1 / squared(WENO_EPS + smooth_one)
    alpha_two = 0.6 / squared(WENO_EPS + smooth_two)
    alpha_three = 0.3 / squared(WENO_EPS + smooth_three)
    weight_sum = alpha_one + alpha_two + alpha_three
    guess_one = far_left / 3.0 - 7.0 * near_left / 6.0 + 11.0 * middle / 6.0
    guess_two = -near_left / 6.0 + 5.0 * middle / 6.0 + near_right / 3.0
    guess_three = middle / 3.0 + 5.0 * near_right / 6.0 - far_right / 6.0
    return (alpha_one * guess_one + alpha_two * guess_two + alpha_three * guess_three) / weight_sum

def one_sided(fetch_at):
    values = [fetch_at(offset) for offset in range(-3, 4)]
    backward = [values[position + 1] - values[position] for position in range(6)]
    minus_side = weno_side(backward[0:5])
    plus_side = weno_side([backward[5], backward[4], backward[3], backward[2], backward[1]])
    return (minus_side, plus_side)

def godunov(minus_side, plus_side, signum):
    growing = jnp.maximum(squared(jnp.maximum(minus_side, 0.0)), squared(jnp.minimum(plus_side, 0.0)))
    shrinking = jnp.maximum(squared(jnp.minimum(minus_side, 0.0)), squared(jnp.maximum(plus_side, 0.0)))
    return jnp.where(signum > 0.0, growing, shrinking)

def rolled(field, along_axis, offset):
    return jnp.roll(field, -offset, along_axis)

def settle_one(field, signum):
    gradient = jnp.zeros_like(field)
    for along_axis in range(3):
        minus_side, plus_side = one_sided(partial(rolled, field, along_axis))
        gradient = gradient + godunov(minus_side, plus_side, signum)
    return field - PSEUDO_STEP * signum * (jnp.sqrt(gradient) - 1.0)

def settle_all(level_pair):
    field, signum = level_pair
    for sweep in range(REINIT):
        field = settle_one(field, signum)
    return field

def local_ranks(level):
    lowest = level[0]
    second = jnp.full_like(lowest, jnp.inf)
    for position in range(1, level.shape[0]):
        second = jnp.minimum(second, jnp.maximum(lowest, level[position]))
        lowest = jnp.minimum(lowest, level[position])
    return (lowest, second)

def project(level, lowest, second):
    other = jnp.where(level == lowest[None], second[None], lowest[None])
    return 0.5 * (level - other)

def reference(grain_ids, colouring, mobility):
    colour_cell = colouring[grain_ids]
    set_index = jnp.arange(SETS, dtype=jnp.int32)[:, None, None, None]
    level = jnp.where(colour_cell[None] == set_index, -0.5, 0.5).astype(jnp.float32)
    for outer_step in range(STEPS):
        laplace = jnp.roll(level, 1, 1) + jnp.roll(level, -1, 1)
        laplace = laplace + jnp.roll(level, 1, 2) + jnp.roll(level, -1, 2)
        laplace = laplace + jnp.roll(level, 1, 3) + jnp.roll(level, -1, 3) - 6.0 * level
        level = level + TIME_STEP * mobility[None] * laplace
        lowest, second = local_ranks(level)
        level = project(level, lowest, second)
        signum = level / jnp.sqrt(level * level + 1.0)
        level = lax.map(settle_all, (level, signum))
    return level
```

```python
import functools

import jax
import jax.numpy as jnp
from jax import lax
from jax.experimental import pallas as pl
from jax.experimental.pallas import tpu as pltpu
from jax.sharding import PartitionSpec as P

SETS = 16
REINIT = 3
HALO = 3
TIME_STEP = 0.08
PSEUDO_STEP = 0.3
WENO_EPS = 1e-06
ROWS = 4
MESH = pl.DeviceIdType.MESH


def turned(value, offset, axis):
    size = value.shape[axis]
    return pltpu.roll(value, (-offset) % size, axis)


def face_sides(diff, second, second_next, third, third_before, third_after, one, two, three):
    p12 = one * two
    p13 = one * three
    p23 = two * three
    p12 = p12 * p12
    p13 = p13 * p13
    p23 = p23 * p23
    u = p23 * (third_before - third)
    v = p12 * (third - third_after)
    both = u + v
    both = both + both
    shared = (p12 + p23) + 6.0 * p13
    minus = (both + v) * pl.reciprocal(shared + (p12 + p12), approx=True)
    plus = (both + u) * pl.reciprocal(shared + (p23 + p23), approx=True)
    diff6 = 6.0 * diff
    ends = second + second_next
    return diff6 + (ends + second_next) + minus, diff6 - (ends + second) - plus


def smoothness(second, third):
    t = third * third
    m = third * second
    a = (4.0 / 3.0) * t + (second * second + WENO_EPS)
    two = a + m
    three = a - m
    tm = t + m
    return two + (tm + tm), two, three


def part_of_gradient(minus, plus, sign):
    side = jnp.maximum(jnp.maximum(sign * minus, -(sign * plus)), 0.0)
    return side * side


def periodic_part(block, sign, axis):
    diff = block - turned(block, -1, axis)
    second = diff - turned(diff, -1, axis)
    second_next = turned(second, 1, axis)
    third = second_next - second
    one_next, two, three_before = smoothness(second, third)
    minus, plus = face_sides(
        diff, second, second_next, third, turned(third, -1, axis), turned(third, 1, axis),
        turned(one_next, -1, axis), two, turned(three_before, 1, axis),
    )
    return part_of_gradient(minus, turned(plus, 1, axis), sign)


def leading_part(window, sign):
    n = sign.shape[0]
    diff = window[1:] - window[:-1]
    second = diff[1:] - diff[:-1]
    third = second[1:] - second[:-1]
    one_next, two, three_before = smoothness(second[:-1], third)
    minus, plus = face_sides(
        diff[2 : n + 3], second[1 : n + 2], second[2 : n + 3], third[1 : n + 2], third[0 : n + 1], third[2 : n + 3],
        one_next[0 : n + 1], two[1 : n + 2], three_before[2 : n + 3],
    )
    return part_of_gradient(minus[:n], plus[1:], sign)


def grow(low, sec, value):
    return jnp.minimum(low, value), jnp.minimum(sec, jnp.maximum(low, value))


def merge(left, right):
    low = jnp.minimum(left[0], right[0])
    sec = jnp.minimum(jnp.maximum(left[0], right[0]), jnp.minimum(left[1], right[1]))
    return low, sec


def projected(level, low, sec):
    return 0.5 * (level - jnp.where(level == low, sec, low))


def kernel(
    sizes, ids_ref, table_ref, mob_ref, out_ref,
    ids, mob, colour, flow, lev, sig, ranks, got_one, half, got_two, final,
    in_send, in_recv, halo_send, halo_recv, set_send, set_recv,
):
    count, near, far, slab_devices, depth = sizes
    group, part, slab = lax.axis_index("groups"), lax.axis_index("set"), lax.axis_index("gy")
    up = lax.rem(slab + slab_devices - 1, slab_devices)
    down = lax.rem(slab + 1, slab_devices)
    low_bit = lax.rem(part, 2)
    sibling = part + 1 - 2 * low_bit
    cross = lax.rem(part + 2, 4)
    to_up, to_down = (group, part, up), (group, part, down)
    to_sibling, to_cross = (group, sibling, slab), (group, cross, slab)

    barrier = pltpu.get_barrier_semaphore()
    for target in (to_up, to_down, to_sibling, to_cross):
        pl.semaphore_signal(barrier, inc=1, device_id=target, device_id_type=MESH)

    for y in range(near):
        ids[far + y] = ids_ref[pl.ds(y, depth, stride=near), :]
        mob[far + y] = TIME_STEP * mob_ref[pl.ds(y, depth, stride=near), :]

    pl.semaphore_wait(barrier, 4)

    def remote(src, dst, send, recv, target):
        return pltpu.make_async_remote_copy(
            src_ref=src, dst_ref=dst, send_sem=send, recv_sem=recv, device_id=target, device_id_type=MESH
        )

    starts = [
        remote(ids.at[pl.ds(far, far)], ids.at[pl.ds(far + near, far)], in_send.at[0], in_recv.at[0], to_up),
        remote(ids.at[pl.ds(near, far)], ids.at[pl.ds(0, far)], in_send.at[1], in_recv.at[1], to_down),
        remote(mob.at[pl.ds(far, HALO)], mob.at[pl.ds(far + near, HALO)], in_send.at[2], in_recv.at[2], to_up),
        remote(mob.at[pl.ds(far + near - HALO, HALO)], mob.at[pl.ds(far - HALO, HALO)], in_send.at[3], in_recv.at[3], to_down),
    ]
    for copy in starts:
        copy.start()

    def colours(first, rows):
        cells = ids[first : first + rows].reshape(rows * depth, 128)
        lane = jnp.bitwise_and(cells, 127)
        line = lax.shift_right_logical(cells, 7)

        def look(at, found):
            entry = jnp.broadcast_to(table_ref[pl.ds(at, 1), :], cells.shape)
            return jnp.where(line == at, jnp.take_along_axis(entry, lane, axis=1), found)

        lines = table_ref.shape[0]
        found = jnp.zeros_like(cells)
        if lines <= 8:
            for at in range(lines):
                found = look(at, found)
        else:
            found = lax.fori_loop(0, lines, look, found)
        colour[first : first + rows] = found.reshape(rows, depth, 128)

    colours(far, near)
    for copy in starts:
        copy.wait()
    colours(0, far)
    colours(far + near, far)

    wide = near + 2 * HALO

    def first_row(y, _):
        def marks(at):
            c = colour[at]
            bit = lax.shift_left(jnp.ones_like(c), 4 * jnp.bitwise_and(c, 7))
            return jnp.where(c < 8, bit, 0), jnp.where(c < 8, 0, bit)

        here = colour[y + 1]
        words = []
        for before, mine, after in zip(marks(y), marks(y + 1), marks(y + 2)):
            words.append(
                before + after + turned(mine, 1, 0) + turned(mine, -1, 0) + turned(mine, 1, 1) + turned(mine, -1, 1)
            )
        pace = mob[y + 1]
        low = sec = None
        for k in range(SETS):
            n = jnp.bitwise_and(lax.shift_right_logical(words[k // 8], 4 * (k % 8)), 7).astype(jnp.float32)
            value = jnp.where(here == k, pace * (6.0 - n) - 0.5, 0.5 - pace * n)
            flow[k, y] = value
            if k == 0:
                low, sec = value, jnp.full_like(value, jnp.inf)
            else:
                low, sec = grow(low, sec, value)
        for i in range(count):
            lev[0, i, y] = projected(flow[part * count + i, y], low, sec)
        return 0

    lax.fori_loop(0, wide, first_row, 0)

    def set_signs():
        def of(i, _):
            def rows(b, _):
                level = lev[0, i, pl.ds(HALO + b * ROWS, ROWS)]
                sig[i, pl.ds(b * ROWS, ROWS)] = level * lax.rsqrt(level * level + 1.0)
                return 0

            return lax.fori_loop(0, near // ROWS, rows, 0)

        lax.fori_loop(0, count, of, 0)

    set_signs()

    def halo_copies(at, k):
        return (
            remote(
                lev.at[at, k, pl.ds(HALO, HALO)], lev.at[at, k, pl.ds(HALO + near, HALO)],
                halo_send.at[at, 0, k], halo_recv.at[at, 0, k], to_up,
            ),
            remote(
                lev.at[at, k, pl.ds(near, HALO)], lev.at[at, k, pl.ds(0, HALO)],
                halo_send.at[at, 1, k], halo_recv.at[at, 1, k], to_down,
            ),
        )

    def send_halo(at, k):
        for copy in halo_copies(at, k):
            copy.start()

    def wait_halo(at, k):
        for copy in halo_copies(at, k):
            copy.wait()

    def sweep(at, wait, last):
        def of(k, _):
            if wait:
                wait_halo(at, k)

            def rows(b, _):
                first = b * ROWS
                window = lev[at, k, pl.ds(first, ROWS + 2 * HALO)]
                signum = sig[k, pl.ds(first, ROWS)]
                sign = jnp.where(signum > 0.0, 1.0, -1.0)
                block = window[HALO : HALO + ROWS]
                gradient = periodic_part(block, sign, 1) + leading_part(window, sign) + periodic_part(block, sign, 2)
                new = block - PSEUDO_STEP * signum * (jnp.sqrt(gradient) * (1.0 / 6.0) - 1.0)
                if last:
                    for y in range(ROWS):
                        out_ref[k, pl.ds(first + y, depth, stride=near), :] = new[y]
                else:
                    lev[1 - at, k, pl.ds(HALO + first, ROWS)] = new
                return 0

            lax.fori_loop(0, near // ROWS, rows, 0)
            if not last:
                send_halo(1 - at, k)
            return 0

        lax.fori_loop(0, count, of, 0)

    sweep(0, False, False)
    sweep(1, True, False)
    sweep(0, True, False)

    for k in range(count):
        wait_halo(1, k)

    def flow_row(y, _):
        pace = mob[far + y]
        low = sec = None
        for k in range(count):
            mine = lev[1, k, HALO + y]
            laplace = turned(mine, 1, 0) + turned(mine, -1, 0) + lev[1, k, HALO + y - 1] + lev[1, k, HALO + y + 1]
            laplace = laplace + turned(mine, 1, 1) + turned(mine, -1, 1) - 6.0 * mine
            value = mine + pace * laplace
            lev[0, k, HALO + y] = value
            if k == 0:
                low, sec = value, jnp.full_like(value, jnp.inf)
            else:
                low, sec = grow(low, sec, value)
        ranks[y, 0] = low
        ranks[y, 1] = sec
        return 0

    lax.fori_loop(0, near, flow_row, 0)

    some = near // 2
    own = low_bit * some
    other = some - own
    first = remote(ranks.at[pl.ds(other, some)], got_one, set_send.at[0], set_recv.at[0], to_sibling)
    first.start()
    first.wait()

    def merge_one(y, _):
        low, sec = merge((ranks[own + y, 0], ranks[own + y, 1]), (got_one[y, 0], got_one[y, 1]))
        half[y, 0] = low
        half[y, 1] = sec
        return 0

    lax.fori_loop(0, some, merge_one, 0)
    second = remote(half, got_two, set_send.at[1], set_recv.at[1], to_cross)
    second.start()
    second.wait()

    def merge_two(y, _):
        low, sec = merge((half[y, 0], half[y, 1]), (got_two[y, 0], got_two[y, 1]))
        final[own + y, 0] = low
        final[own + y, 1] = sec
        return 0

    lax.fori_loop(0, some, merge_two, 0)
    third = remote(final.at[pl.ds(own, some)], final.at[pl.ds(own, some)], set_send.at[2], set_recv.at[2], to_sibling)
    third.start()
    third.wait()

    def project_of(k, _):
        def row(y, _):
            lev[0, k, HALO + y] = projected(lev[0, k, HALO + y], final[y, 0], final[y, 1])
            return 0

        lax.fori_loop(0, near, row, 0)
        send_halo(0, k)
        return 0

    lax.fori_loop(0, count, project_of, 0)
    set_signs()

    sweep(0, True, False)
    sweep(1, True, False)
    sweep(0, True, True)


def solution(mesh):
    slab_devices = mesh.shape["gy"]
    count = SETS // mesh.shape["set"]

    def shards(grain_ids, colouring, mobility):
        depth, near, width = grain_ids.shape
        far = HALO + 1
        wide = near + 2 * HALO
        tile = (depth, width)
        out = pl.pallas_call(
            functools.partial(kernel, (count, near, far, slab_devices, depth)),
            out_shape=jax.ShapeDtypeStruct((count, depth * near, width), jnp.float32),
            in_specs=[pl.BlockSpec(memory_space=pltpu.VMEM)] * 3,
            out_specs=pl.BlockSpec(memory_space=pltpu.VMEM),
            scratch_shapes=[
                pltpu.VMEM((near + 2 * far,) + tile, jnp.int32),
                pltpu.VMEM((near + 2 * far,) + tile, jnp.float32),
                pltpu.VMEM((near + 2 * far,) + tile, jnp.int32),
                pltpu.VMEM((SETS, wide) + tile, jnp.float32),
                pltpu.VMEM((2, count, wide) + tile, jnp.float32),
                pltpu.VMEM((count, near) + tile, jnp.float32),
                pltpu.VMEM((near, 2) + tile, jnp.float32),
                pltpu.VMEM((near // 2, 2) + tile, jnp.float32),
                pltpu.VMEM((near // 2, 2) + tile, jnp.float32),
                pltpu.VMEM((near // 2, 2) + tile, jnp.float32),
                pltpu.VMEM((near, 2) + tile, jnp.float32),
                pltpu.SemaphoreType.DMA((4,)),
                pltpu.SemaphoreType.DMA((4,)),
                pltpu.SemaphoreType.DMA((2, 2, count)),
                pltpu.SemaphoreType.DMA((2, 2, count)),
                pltpu.SemaphoreType.DMA((3,)),
                pltpu.SemaphoreType.DMA((3,)),
            ],
            compiler_params=pltpu.CompilerParams(
                collective_id=0, has_side_effects=True, vmem_limit_bytes=32 * 1024 * 1024
            ),
        )(
            grain_ids.reshape(depth * near, width),
            colouring.reshape(-1, width),
            mobility.reshape(depth * near, width),
        )
        return out.reshape(count, depth, near, width)

    return jax.shard_map(
        shards,
        mesh=mesh,
        in_specs=(P("groups", "gy", None), P("groups"), P("groups", "gy", None)),
        out_specs=P(("groups", "set"), None, "gy", None),
        check_vma=False,
    )
```

```python
import functools

import jax
import jax.numpy as jnp
from jax import lax
from jax.experimental import pallas as pl
from jax.experimental.pallas import tpu as pltpu
from jax.sharding import PartitionSpec as P

SETS = 16
REINIT = 3
HALO = 3
TIME_STEP = 0.08
PSEUDO_STEP = 0.3
WENO_EPS = 1e-06
WIDER = 2 * HALO
MESH = pl.DeviceIdType.MESH


def turned(value, offset, axis):
    size = value.shape[axis]
    return pltpu.roll(value, (-offset) % size, axis)


def face_sides(diff, second, second_next, third, third_before, third_after, one, two, three):
    p12 = one * two
    p13 = one * three
    p23 = two * three
    p12 = p12 * p12
    p13 = p13 * p13
    p23 = p23 * p23
    u = p23 * (third_before - third)
    v = p12 * (third - third_after)
    both = u + v
    both = both + both
    shared = (p12 + p23) + 6.0 * p13
    minus = (both + v) * pl.reciprocal(shared + (p12 + p12), approx=True)
    plus = (both + u) * pl.reciprocal(shared + (p23 + p23), approx=True)
    diff6 = 6.0 * diff
    ends = second + second_next
    return diff6 + (ends + second_next) + minus, diff6 - (ends + second) - plus


def smoothness(second, third):
    t = third * third
    m = third * second
    a = (4.0 / 3.0) * t + (second * second + WENO_EPS)
    two = a + m
    three = a - m
    tm = t + m
    return two + (tm + tm), two, three


def part_of_gradient(minus, plus, sign):
    side = jnp.maximum(jnp.maximum(sign * minus, -(sign * plus)), 0.0)
    return side * side


def periodic_part(block, sign, axis):
    diff = block - turned(block, -1, axis)
    second = diff - turned(diff, -1, axis)
    second_next = turned(second, 1, axis)
    third = second_next - second
    third_before, third_after = turned(third, -1, axis), turned(third, 1, axis)
    if axis == 1:
        one_next, two, three_before = smoothness(second, third)
        one, three = turned(one_next, -1, axis), turned(three_before, 1, axis)
    else:
        here = second * second + WENO_EPS
        one = third_before * ((4.0 / 3.0) * third_before + second) + here
        two = third * ((4.0 / 3.0) * third + second) + here
        three = third_after * ((4.0 / 3.0) * third_after - second_next) + (second_next * second_next + WENO_EPS)
    minus, plus = face_sides(diff, second, second_next, third, third_before, third_after, one, two, three)
    return part_of_gradient(minus, turned(plus, 1, axis), sign)


def leading_part(window, sign):
    n = sign.shape[0]
    diff = window[1:] - window[:-1]
    second = diff[1:] - diff[:-1]
    third = second[1:] - second[:-1]
    one_next, two, three_before = smoothness(second[:-1], third)
    minus, plus = face_sides(
        diff[2 : n + 3], second[1 : n + 2], second[2 : n + 3], third[1 : n + 2], third[0 : n + 1], third[2 : n + 3],
        one_next[0 : n + 1], two[1 : n + 2], three_before[2 : n + 3],
    )
    return part_of_gradient(minus[:n], plus[1:], sign)


def grow(low, sec, value):
    return jnp.minimum(low, value), jnp.minimum(sec, jnp.maximum(low, value))


def merge(left, right):
    low = jnp.minimum(left[0], right[0])
    sec = jnp.minimum(jnp.maximum(left[0], right[0]), jnp.minimum(left[1], right[1]))
    return low, sec


def projected(level, low, sec):
    return 0.5 * (level - jnp.where(level == low, sec, low))


def kernel(
    sizes, ids_ref, table_ref, mob_ref, out_ref,
    ids, mob, colour, flow, lev, sig, ranks, got_one, half, got_two, final,
    ids_in, mob_in, table, load_sem, in_send, in_recv, halo_send, halo_recv, set_send, set_recv,
):
    count, near, far, slab_devices, depth = sizes
    group, part, slab = lax.axis_index("groups"), lax.axis_index("set"), lax.axis_index("gy")
    up = lax.rem(slab + slab_devices - 1, slab_devices)
    down = lax.rem(slab + 1, slab_devices)
    low_bit = lax.rem(part, 2)
    sibling = part + 1 - 2 * low_bit
    cross = lax.rem(part + 2, 4)
    to_up, to_down = (group, part, up), (group, part, down)
    to_sibling, to_cross = (group, sibling, slab), (group, cross, slab)

    barrier = pltpu.get_barrier_semaphore()
    for target in (to_up, to_down, to_sibling, to_cross):
        pl.semaphore_signal(barrier, inc=1, device_id=target, device_id_type=MESH)

    loads = [
        pltpu.make_async_copy(ids_ref, ids_in, load_sem.at[0]),
        pltpu.make_async_copy(mob_ref, mob_in, load_sem.at[1]),
        pltpu.make_async_copy(table_ref, table, load_sem.at[2]),
    ]
    for copy in loads:
        copy.start()
    for copy in loads:
        copy.wait()
    for y in range(near):
        ids[far + y] = ids_in[pl.ds(y, depth, stride=near), :]
        mob[far + y] = TIME_STEP * mob_in[pl.ds(y, depth, stride=near), :]

    pl.semaphore_wait(barrier, 4)

    def remote(src, dst, send, recv, target):
        return pltpu.make_async_remote_copy(
            src_ref=src, dst_ref=dst, send_sem=send, recv_sem=recv, device_id=target, device_id_type=MESH
        )

    starts = [
        remote(ids.at[pl.ds(far, far)], ids.at[pl.ds(far + near, far)], in_send.at[0], in_recv.at[0], to_up),
        remote(ids.at[pl.ds(near, far)], ids.at[pl.ds(0, far)], in_send.at[1], in_recv.at[1], to_down),
        remote(mob.at[pl.ds(far, WIDER)], mob.at[pl.ds(far + near, WIDER)], in_send.at[2], in_recv.at[2], to_up),
        remote(mob.at[pl.ds(far + near - WIDER, WIDER)], mob.at[pl.ds(far - WIDER, WIDER)], in_send.at[3], in_recv.at[3], to_down),
    ]
    for copy in starts:
        copy.start()

    def colours(first, rows):
        cells = ids[first : first + rows].reshape(rows * depth, 128)
        lane = jnp.bitwise_and(cells, 127)
        line = lax.shift_right_logical(cells, 7)

        def look(at, found):
            entry = jnp.broadcast_to(table[pl.ds(at, 1), :], cells.shape)
            return jnp.where(line == at, jnp.take_along_axis(entry, lane, axis=1), found)

        lines = table.shape[0]
        found = jnp.zeros_like(cells)
        if lines <= 8:
            for at in range(lines):
                found = look(at, found)
        else:
            found = lax.fori_loop(0, lines, look, found)
        colour[first : first + rows] = found.reshape(rows, depth, 128)

    colours(far, near)

    wide = near + 2 * WIDER

    inner = (near - 2) // 2

    def settle(i, rows, value, low, sec):
        level = projected(value, low, sec)
        lev[0, i, pl.ds(rows.start + 1, rows.size)] = level
        sig[i, rows] = level * lax.rsqrt(level * level + 1.0)

    def first_rows(y, n):
        c = colour[pl.ds(y, n + 2)]
        bit = lax.shift_left(jnp.ones_like(c), 4 * jnp.bitwise_and(c, 7))
        here = c[1 : n + 1]
        words = []
        for marks in (jnp.where(c < 8, bit, 0), jnp.where(c < 8, 0, bit)):
            mine = marks[1 : n + 1]
            words.append(
                marks[:n] + marks[2:] + turned(mine, 1, 1) + turned(mine, -1, 1) + turned(mine, 1, 2) + turned(mine, -1, 2)
            )
        pace = mob[pl.ds(y + 1, n)]
        low = sec = None
        for k in range(SETS):
            faces = jnp.bitwise_and(lax.shift_right_logical(words[k // 8], 4 * (k % 8)), 7).astype(jnp.float32)
            value = jnp.where(here == k, pace * (6.0 - faces) - 0.5, 0.5 - pace * faces)
            flow[k, pl.ds(y, n)] = value
            if k == 0:
                low, sec = value, jnp.full_like(value, jnp.inf)
            else:
                low, sec = grow(low, sec, value)
        for i in range(count):
            settle(i, pl.ds(y, n), flow[part * count + i, pl.ds(y, n)], low, sec)

    def inner_rows(of):
        def block(b, _):
            of(far + b * inner, inner)
            return 0

        lax.fori_loop(0, 2, block, 0)

    def outer_rows(of):
        def block(b, _):
            of(b * (wide - far), far)
            return 0

        lax.fori_loop(0, 2, block, 0)

    inner_rows(first_rows)
    for copy in starts:
        copy.wait_recv()
    colours(0, far)
    colours(far + near, far)
    outer_rows(first_rows)

    def halo_copies(message, at, k, rows):
        return (
            remote(
                lev.at[at, k, pl.ds(far, rows)], lev.at[at, k, pl.ds(far + near, rows)],
                halo_send.at[message, 0, k], halo_recv.at[message, 0, k], to_up,
            ),
            remote(
                lev.at[at, k, pl.ds(far + near - rows, rows)], lev.at[at, k, pl.ds(far - rows, rows)],
                halo_send.at[message, 1, k], halo_recv.at[message, 1, k], to_down,
            ),
        )

    def send_halo(*message):
        for copy in halo_copies(*message):
            copy.start()

    def wait_halo(*message):
        for copy in halo_copies(*message):
            copy.wait_recv()

    def wait_sent(*message):
        for copy in halo_copies(*message):
            copy.wait_send()

    def sweep(at, to, k, margin):
        rows = near + 2 * margin
        window = lev[at, k, pl.ds(far - margin - HALO, rows + 2 * HALO)]
        signum = sig[k, pl.ds(WIDER - margin, rows)]
        sign = jnp.where(signum > 0.0, 1.0, -1.0)
        block = window[HALO : HALO + rows]
        gradient = periodic_part(block, sign, 1) + leading_part(window, sign) + periodic_part(block, sign, 2)
        new = block - PSEUDO_STEP * signum * (jnp.sqrt(gradient) * (1.0 / 6.0) - 1.0)
        if to is None:
            for y in range(near):
                out_ref[k, pl.ds(y, depth, stride=near), :] = new[y]
        else:
            lev[to, k, pl.ds(far - margin, rows)] = new

    def step_one(k, _):
        sweep(0, 1, k, HALO)
        sweep(1, 2, k, 0)
        send_halo(0, 2, k, HALO)
        return 0

    def step_one_end(k, _):
        wait_halo(0, 2, k, HALO)
        sweep(2, 1, k, 0)
        send_halo(1, 1, k, far)
        return 0

    lax.fori_loop(0, count, step_one, 0)
    lax.fori_loop(0, count, step_one_end, 0)

    def flow_rows(y, n):
        pace = mob[pl.ds(y + 1, n)]
        low = sec = None
        for k in range(count):
            window = lev[1, k, pl.ds(y, n + 2)]
            mine = window[1 : n + 1]
            laplace = turned(mine, 1, 1) + turned(mine, -1, 1) + window[:n] + window[2:]
            laplace = laplace + turned(mine, 1, 2) + turned(mine, -1, 2) - 6.0 * mine
            value = mine + pace * laplace
            lev[0, k, pl.ds(y + 1, n)] = value
            if k == 0:
                low, sec = value, jnp.full_like(value, jnp.inf)
            else:
                low, sec = grow(low, sec, value)
        ranks[0, pl.ds(y, n)] = low
        ranks[1, pl.ds(y, n)] = sec

    inner_rows(flow_rows)
    for k in range(count):
        wait_halo(1, 1, k, far)
    outer_rows(flow_rows)

    some = wide // 2
    own = low_bit * some
    other = some - own
    mine, theirs = pl.ds(own, some), pl.ds(other, some)
    first = remote(ranks.at[:, theirs], got_one, set_send.at[0], set_recv.at[0], to_sibling)
    first.start()
    first.wait_recv()
    half[0], half[1] = merge((ranks[0, mine], ranks[1, mine]), (got_one[0], got_one[1]))
    second = remote(half, got_two, set_send.at[1], set_recv.at[1], to_cross)
    second.start()
    second.wait_recv()

    final[0, mine], final[1, mine] = merge((half[0], half[1]), (got_two[0], got_two[1]))
    third = remote(final.at[:, mine], final.at[:, mine], set_send.at[2], set_recv.at[2], to_sibling)
    third.start()
    third.wait_recv()

    def step_two(k, _):
        wait_sent(1, 1, k, far)
        settle(k, pl.ds(0, wide), lev[0, k, pl.ds(1, wide)], final[0], final[1])
        sweep(0, 1, k, HALO)
        wait_sent(0, 2, k, HALO)
        sweep(1, 2, k, 0)
        send_halo(2, 2, k, HALO)
        return 0

    def step_two_end(k, _):
        wait_halo(2, 2, k, HALO)
        sweep(2, None, k, 0)
        wait_sent(2, 2, k, HALO)
        return 0

    lax.fori_loop(0, count, step_two, 0)
    lax.fori_loop(0, count, step_two_end, 0)
    for copy in starts + [first, second, third]:
        copy.wait_send()


def solution(mesh):
    slab_devices = mesh.shape["gy"]
    count = SETS // mesh.shape["set"]

    def shards(grain_ids, colouring, mobility):
        depth, near, width = grain_ids.shape
        far = WIDER + 1
        wide = near + 2 * WIDER
        tile = (depth, width)
        out = pl.pallas_call(
            functools.partial(kernel, (count, near, far, slab_devices, depth)),
            out_shape=jax.ShapeDtypeStruct((count, depth * near, width), jnp.float32),
            in_specs=[pl.BlockSpec(memory_space=pltpu.HBM)] * 3,
            out_specs=pl.BlockSpec(memory_space=pltpu.VMEM),
            scratch_shapes=[
                pltpu.VMEM((near + 2 * far,) + tile, jnp.int32),
                pltpu.VMEM((near + 2 * far,) + tile, jnp.float32),
                pltpu.VMEM((near + 2 * far,) + tile, jnp.int32),
                pltpu.VMEM((SETS, wide) + tile, jnp.float32),
                pltpu.VMEM((3, count, near + 2 * far) + tile, jnp.float32),
                pltpu.VMEM((count, wide) + tile, jnp.float32),
                pltpu.VMEM((2, wide) + tile, jnp.float32),
                pltpu.VMEM((2, wide // 2) + tile, jnp.float32),
                pltpu.VMEM((2, wide // 2) + tile, jnp.float32),
                pltpu.VMEM((2, wide // 2) + tile, jnp.float32),
                pltpu.VMEM((2, wide) + tile, jnp.float32),
                pltpu.VMEM((depth * near, width), jnp.int32),
                pltpu.VMEM((depth * near, width), jnp.float32),
                pltpu.VMEM((colouring.size // width, width), jnp.int32),
                pltpu.SemaphoreType.DMA((3,)),
                pltpu.SemaphoreType.DMA((4,)),
                pltpu.SemaphoreType.DMA((4,)),
                pltpu.SemaphoreType.DMA((3, 2, count)),
                pltpu.SemaphoreType.DMA((3, 2, count)),
                pltpu.SemaphoreType.DMA((3,)),
                pltpu.SemaphoreType.DMA((3,)),
            ],
            compiler_params=pltpu.CompilerParams(
                collective_id=0, has_side_effects=True
            ),
        )(
            grain_ids.reshape(depth * near, width),
            colouring.reshape(-1, width),
            mobility.reshape(depth * near, width),
        )
        return out.reshape(count, depth, near, width)

    return jax.shard_map(
        shards,
        mesh=mesh,
        in_specs=(P("groups", "gy", None), P("groups"), P("groups", "gy", None)),
        out_specs=P(("groups", "set"), None, "gy", None),
        check_vma=False,
    )
```

```python
import functools

import jax
import jax.numpy as jnp
from jax import lax
from jax.experimental import pallas as pl
from jax.experimental.pallas import tpu as pltpu
from jax.sharding import PartitionSpec as P

SETS = 16
REINIT = 3
HALO = 3
TIME_STEP = 0.08
PSEUDO_STEP = 0.3
WENO_EPS = 1e-06
WIDER = 2 * HALO
MESH = pl.DeviceIdType.MESH


def turned(value, offset, axis):
    size = value.shape[axis]
    return pltpu.roll(value, (-offset) % size, axis)


def face_sides(diff, second, second_next, third, third_before, third_after, one, two, three):
    p12 = one * two
    p13 = one * three
    p23 = two * three
    p12 = p12 * p12
    p13 = p13 * p13
    p23 = p23 * p23
    u = p23 * (third_before - third)
    v = p12 * (third - third_after)
    both = u + v
    both = both + both
    shared = (p12 + p23) + 6.0 * p13
    minus = (both + v) * pl.reciprocal(shared + (p12 + p12), approx=True)
    plus = (both + u) * pl.reciprocal(shared + (p23 + p23), approx=True)
    diff6 = 6.0 * diff
    ends = second + second_next
    return diff6 + (ends + second_next) + minus, diff6 - (ends + second) - plus


def smoothness(second, third):
    t = third * third
    m = third * second
    a = (4.0 / 3.0) * t + (second * second + WENO_EPS)
    two = a + m
    three = a - m
    tm = t + m
    return two + (tm + tm), two, three


def part_of_gradient(minus, plus, sign):
    side = jnp.maximum(jnp.maximum(sign * minus, -(sign * plus)), 0.0)
    return side * side


def periodic_part(block, sign, axis):
    diff = block - turned(block, -1, axis)
    second = diff - turned(diff, -1, axis)
    second_next = turned(second, 1, axis)
    third = second_next - second
    third_before, third_after = turned(third, -1, axis), turned(third, 1, axis)
    if axis == 1:
        one_next, two, three_before = smoothness(second, third)
        one, three = turned(one_next, -1, axis), turned(three_before, 1, axis)
    else:
        here = second * second + WENO_EPS
        one = third_before * ((4.0 / 3.0) * third_before + second) + here
        two = third * ((4.0 / 3.0) * third + second) + here
        three = third_after * ((4.0 / 3.0) * third_after - second_next) + (second_next * second_next + WENO_EPS)
    minus, plus = face_sides(diff, second, second_next, third, third_before, third_after, one, two, three)
    return part_of_gradient(minus, turned(plus, 1, axis), sign)


def leading_part(window, sign):
    n = sign.shape[0]
    diff = window[1:] - window[:-1]
    second = diff[1:] - diff[:-1]
    third = second[1:] - second[:-1]
    one_next, two, three_before = smoothness(second[:-1], third)
    minus, plus = face_sides(
        diff[2 : n + 3], second[1 : n + 2], second[2 : n + 3], third[1 : n + 2], third[0 : n + 1], third[2 : n + 3],
        one_next[0 : n + 1], two[1 : n + 2], three_before[2 : n + 3],
    )
    return part_of_gradient(minus[:n], plus[1:], sign)


def grow(low, sec, value):
    return jnp.minimum(low, value), jnp.minimum(sec, jnp.maximum(low, value))


def merge(left, right):
    low = jnp.minimum(left[0], right[0])
    sec = jnp.minimum(jnp.maximum(left[0], right[0]), jnp.minimum(left[1], right[1]))
    return low, sec


def projected(level, low, sec):
    return 0.5 * (level - jnp.where(level == low, sec, low))


def kernel(
    sizes, ids_ref, table_ref, mob_ref, out_ref,
    ids, mob, colour, flow, lev, sig, ranks, got_one, half, got_two, final,
    ids_in, mob_in, table, load_sem, in_send, in_recv, halo_send, halo_recv, set_send, set_recv,
):
    count, near, far, slab_devices, depth = sizes
    group, part, slab = lax.axis_index("groups"), lax.axis_index("set"), lax.axis_index("gy")
    up = lax.rem(slab + slab_devices - 1, slab_devices)
    down = lax.rem(slab + 1, slab_devices)
    low_bit = lax.rem(part, 2)
    sibling = part + 1 - 2 * low_bit
    cross = lax.rem(part + 2, 4)
    to_up, to_down = (group, part, up), (group, part, down)
    to_sibling, to_cross = (group, sibling, slab), (group, cross, slab)

    barrier = pltpu.get_barrier_semaphore()
    for target in (to_up, to_down, to_sibling, to_cross):
        pl.semaphore_signal(barrier, inc=1, device_id=target, device_id_type=MESH)

    loads = [
        pltpu.make_async_copy(ids_ref, ids_in, load_sem.at[0]),
        pltpu.make_async_copy(mob_ref, mob_in, load_sem.at[1]),
        pltpu.make_async_copy(table_ref, table, load_sem.at[2]),
    ]
    for copy in loads:
        copy.start()
    for copy in loads:
        copy.wait()
    for y in range(near):
        ids[far + y] = ids_in[pl.ds(y, depth, stride=near), :]
        mob[far + y] = TIME_STEP * mob_in[pl.ds(y, depth, stride=near), :]

    pl.semaphore_wait(barrier, 4)

    def remote(src, dst, send, recv, target):
        return pltpu.make_async_remote_copy(
            src_ref=src, dst_ref=dst, send_sem=send, recv_sem=recv, device_id=target, device_id_type=MESH
        )

    starts = [
        remote(ids.at[pl.ds(far, far)], ids.at[pl.ds(far + near, far)], in_send.at[0], in_recv.at[0], to_up),
        remote(ids.at[pl.ds(near, far)], ids.at[pl.ds(0, far)], in_send.at[1], in_recv.at[1], to_down),
        remote(mob.at[pl.ds(far, WIDER)], mob.at[pl.ds(far + near, WIDER)], in_send.at[2], in_recv.at[2], to_up),
        remote(mob.at[pl.ds(far + near - WIDER, WIDER)], mob.at[pl.ds(far - WIDER, WIDER)], in_send.at[3], in_recv.at[3], to_down),
    ]
    for copy in starts:
        copy.start()

    def colours(first, rows):
        cells = ids[first : first + rows].reshape(rows * depth, 128)
        lane = jnp.bitwise_and(cells, 127)
        line = lax.shift_right_logical(cells, 7)

        def look(at, found):
            entry = jnp.broadcast_to(table[pl.ds(at, 1), :], cells.shape)
            return jnp.where(line == at, jnp.take_along_axis(entry, lane, axis=1), found)

        lines = table.shape[0]
        found = jnp.zeros_like(cells)
        if lines <= 8:
            for at in range(lines):
                found = look(at, found)
        else:
            found = lax.fori_loop(0, lines, look, found)
        colour[first : first + rows] = found.reshape(rows, depth, 128)

    colours(far, near)

    wide = near + 2 * WIDER

    inner = (near - 2) // 2

    def settle(i, rows, value, low, sec):
        level = projected(value, low, sec)
        lev[0, i, pl.ds(rows.start + 1, rows.size)] = level
        sig[i, rows] = level * lax.rsqrt(level * level + 1.0)

    def first_rows(y, n):
        c = colour[pl.ds(y, n + 2)]
        bit = lax.shift_left(jnp.ones_like(c), 4 * jnp.bitwise_and(c, 7))
        here = c[1 : n + 1]
        words = []
        for marks in (jnp.where(c < 8, bit, 0), jnp.where(c < 8, 0, bit)):
            mine = marks[1 : n + 1]
            words.append(
                marks[:n] + marks[2:] + turned(mine, 1, 1) + turned(mine, -1, 1) + turned(mine, 1, 2) + turned(mine, -1, 2)
            )
        pace = mob[pl.ds(y + 1, n)]
        low = sec = None
        for k in range(SETS):
            faces = jnp.bitwise_and(lax.shift_right_logical(words[k // 8], 4 * (k % 8)), 7).astype(jnp.float32)
            value = jnp.where(here == k, pace * (6.0 - faces) - 0.5, 0.5 - pace * faces)
            flow[k, pl.ds(y, n)] = value
            if k == 0:
                low, sec = value, jnp.full_like(value, jnp.inf)
            else:
                low, sec = grow(low, sec, value)
        for i in range(count):
            settle(i, pl.ds(y, n), flow[part * count + i, pl.ds(y, n)], low, sec)

    def inner_rows(of):
        def block(b, _):
            of(far + b * inner, inner)
            return 0

        lax.fori_loop(0, 2, block, 0)

    def outer_rows(of):
        def block(b, _):
            of(b * (wide - far), far)
            return 0

        lax.fori_loop(0, 2, block, 0)

    inner_rows(first_rows)
    for copy in starts:
        copy.wait_recv()
    colours(0, far)
    colours(far + near, far)
    outer_rows(first_rows)

    def halo_copies(message, at, k, rows):
        return (
            remote(
                lev.at[at, k, pl.ds(far, rows)], lev.at[at, k, pl.ds(far + near, rows)],
                halo_send.at[message, 0, k], halo_recv.at[message, 0, k], to_up,
            ),
            remote(
                lev.at[at, k, pl.ds(far + near - rows, rows)], lev.at[at, k, pl.ds(far - rows, rows)],
                halo_send.at[message, 1, k], halo_recv.at[message, 1, k], to_down,
            ),
        )

    def send_halo(*message):
        for copy in halo_copies(*message):
            copy.start()

    def wait_halo(*message):
        for copy in halo_copies(*message):
            copy.wait_recv()

    def wait_sent(*message):
        for copy in halo_copies(*message):
            copy.wait_send()

    def sweep(at, to, k, margin):
        rows = near + 2 * margin
        window = lev[at, k, pl.ds(far - margin - HALO, rows + 2 * HALO)]
        signum = sig[k, pl.ds(WIDER - margin, rows)]
        sign = jnp.where(signum > 0.0, 1.0, -1.0)
        block = window[HALO : HALO + rows]
        gradient = periodic_part(block, sign, 1) + leading_part(window, sign) + periodic_part(block, sign, 2)
        new = block - PSEUDO_STEP * signum * (jnp.sqrt(gradient) * (1.0 / 6.0) - 1.0)
        if to is None:
            for y in range(near):
                out_ref[k, pl.ds(y, depth, stride=near), :] = new[y]
        else:
            lev[to, k, pl.ds(far - margin, rows)] = new

    def step_one(k, _):
        sweep(0, 1, k, HALO)
        sweep(1, 2, k, 0)
        send_halo(0, 2, k, HALO)
        return 0

    def step_one_end(k, _):
        wait_halo(0, 2, k, HALO)
        sweep(2, 1, k, 0)
        send_halo(1, 1, k, far)
        return 0

    lax.fori_loop(0, count, step_one, 0)
    lax.fori_loop(0, count, step_one_end, 0)

    def flow_rows(y, n):
        pace = mob[pl.ds(y + 1, n)]
        low = sec = None
        for k in range(count):
            window = lev[1, k, pl.ds(y, n + 2)]
            mine = window[1 : n + 1]
            laplace = turned(mine, 1, 1) + turned(mine, -1, 1) + window[:n] + window[2:]
            laplace = laplace + turned(mine, 1, 2) + turned(mine, -1, 2) - 6.0 * mine
            value = mine + pace * laplace
            lev[0, k, pl.ds(y + 1, n)] = value
            if k == 0:
                low, sec = value, jnp.full_like(value, jnp.inf)
            else:
                low, sec = grow(low, sec, value)
        ranks[0, pl.ds(y, n)] = low
        ranks[1, pl.ds(y, n)] = sec

    def join(turn, n, start):
        mine, theirs = pl.ds(start(low_bit), n), pl.ds(start(1 - low_bit), n)
        here = pl.ds(0, n)
        first = remote(
            ranks.at[:, theirs], got_one.at[turn, :, here], set_send.at[turn, 0], set_recv.at[turn, 0], to_sibling
        )
        first.start()
        yield
        first.wait_recv()
        half[turn, 0, here], half[turn, 1, here] = merge(
            (ranks[0, mine], ranks[1, mine]), (got_one[turn, 0, here], got_one[turn, 1, here])
        )
        second = remote(
            half.at[turn, :, here], got_two.at[turn, :, here], set_send.at[turn, 1], set_recv.at[turn, 1], to_cross
        )
        second.start()
        yield
        second.wait_recv()
        final[0, mine], final[1, mine] = merge(
            (half[turn, 0, here], half[turn, 1, here]), (got_two[turn, 0, here], got_two[turn, 1, here])
        )
        third = remote(final.at[:, mine], final.at[:, mine], set_send.at[turn, 2], set_recv.at[turn, 2], to_sibling)
        third.start()
        yield
        third.wait_recv()
        joins.extend([first, second, third])
        yield

    inner_rows(flow_rows)
    joins = []
    inner_join = join(0, inner, lambda b: far + b * inner)
    outer_join = join(1, far, lambda b: b * (wide - far))
    next(inner_join)
    next(inner_join)
    for k in range(count):
        wait_halo(1, 1, k, far)
    outer_rows(flow_rows)
    for step in (outer_join, inner_join, outer_join, outer_join, inner_join, outer_join):
        next(step)

    def step_two(k, _):
        wait_sent(1, 1, k, far)
        settle(k, pl.ds(0, wide), lev[0, k, pl.ds(1, wide)], final[0], final[1])
        sweep(0, 1, k, HALO)
        wait_sent(0, 2, k, HALO)
        sweep(1, 2, k, 0)
        send_halo(2, 2, k, HALO)
        return 0

    def step_two_end(k, _):
        wait_halo(2, 2, k, HALO)
        sweep(2, None, k, 0)
        wait_sent(2, 2, k, HALO)
        return 0

    lax.fori_loop(0, count, step_two, 0)
    lax.fori_loop(0, count, step_two_end, 0)
    for copy in starts + joins:
        copy.wait_send()


def solution(mesh):
    slab_devices = mesh.shape["gy"]
    count = SETS // mesh.shape["set"]

    def shards(grain_ids, colouring, mobility):
        depth, near, width = grain_ids.shape
        far = WIDER + 1
        wide = near + 2 * WIDER
        tile = (depth, width)
        out = pl.pallas_call(
            functools.partial(kernel, (count, near, far, slab_devices, depth)),
            out_shape=jax.ShapeDtypeStruct((count, depth * near, width), jnp.float32),
            in_specs=[pl.BlockSpec(memory_space=pltpu.HBM)] * 3,
            out_specs=pl.BlockSpec(memory_space=pltpu.VMEM),
            scratch_shapes=[
                pltpu.VMEM((near + 2 * far,) + tile, jnp.int32),
                pltpu.VMEM((near + 2 * far,) + tile, jnp.float32),
                pltpu.VMEM((near + 2 * far,) + tile, jnp.int32),
                pltpu.VMEM((SETS, wide) + tile, jnp.float32),
                pltpu.VMEM((3, count, near + 2 * far) + tile, jnp.float32),
                pltpu.VMEM((count, wide) + tile, jnp.float32),
                pltpu.VMEM((2, wide) + tile, jnp.float32),
                pltpu.VMEM((2, 2, far) + tile, jnp.float32),
                pltpu.VMEM((2, 2, far) + tile, jnp.float32),
                pltpu.VMEM((2, 2, far) + tile, jnp.float32),
                pltpu.VMEM((2, wide) + tile, jnp.float32),
                pltpu.VMEM((depth * near, width), jnp.int32),
                pltpu.VMEM((depth * near, width), jnp.float32),
                pltpu.VMEM((colouring.size // width, width), jnp.int32),
                pltpu.SemaphoreType.DMA((3,)),
                pltpu.SemaphoreType.DMA((4,)),
                pltpu.SemaphoreType.DMA((4,)),
                pltpu.SemaphoreType.DMA((3, 2, count)),
                pltpu.SemaphoreType.DMA((3, 2, count)),
                pltpu.SemaphoreType.DMA((2, 3)),
                pltpu.SemaphoreType.DMA((2, 3)),
            ],
            compiler_params=pltpu.CompilerParams(
                collective_id=0, has_side_effects=True
            ),
        )(
            grain_ids.reshape(depth * near, width),
            colouring.reshape(-1, width),
            mobility.reshape(depth * near, width),
        )
        return out.reshape(count, depth, near, width)

    return jax.shard_map(
        shards,
        mesh=mesh,
        in_specs=(P("groups", "gy", None), P("groups"), P("groups", "gy", None)),
        out_specs=P(("groups", "set"), None, "gy", None),
        check_vma=False,
    )
```
